256 devices in a mesh: aux: 64 (over z, x, core), pair: 4 (over y).
Axes of the slice: x: 4, y: 4, z: 8, core: 2. Of those that a mesh axis runs over, the one named last changes fastest.
Arguments:
- three_center: float32 [65536, 4, 384], P('aux', 'pair'), may hold values from -1 to 1
- occ_energy: float32 [4], P('pair'), may hold values from -1.5 to -0.3
- vir_energy: float32 [384], replicated, may hold values from 0.2 to 3
- pair_mask: int32 [4, 4], replicated, may hold values from 0 to 1, as said below
Outputs:
- gamma_aux: float32 [65536, 4, 384], P('aux', 'pair')
The draws below stay inside these ranges and needn't reach their ends.
Inputs may be any that keep to these rules, and one draw needn't show every extreme that they name: pair_mask is symmetric and holds 1 on its diagonal.
All inputs are finite; a program needn't handle non-finite values.
Results may differ from the reference program's by a relative error of at most 0.000071.
Values sent between devices are 32-bit elements; how exact they have to be, the bound alone decides.
A program may use at most 64 MiB of HBM per device.

```python
import jax
import jax.numpy as jnp
from jax import lax

VIR = 384
OCC_DEV = 1
NAUX = 65536
NOCC = 4


def draw_pair_mask(key, part):
    first_key, second_key = jax.random.split(jax.random.fold_in(key, 17))
    panel_count = NOCC // OCC_DEV
    levels = jax.random.randint(first_key, (panel_count,), 0, 4)
    orbital_panel = jnp.arange(NOCC, dtype=jnp.int32) // OCC_DEV
    level_rows = levels[orbital_panel]
    cutoff = level_rows[:, None] + level_rows[None, :]
    uniform_ints = jax.random.randint(second_key, (NOCC, NOCC), 0, 7)
    upper_part = (uniform_ints < cutoff).astype(jnp.int32)
    orbital_index = jnp.arange(NOCC, dtype=jnp.int32)
    symmetric = jnp.where(orbital_index[:, None] <= orbital_index[None, :], upper_part, upper_part.T)
    return jnp.where(orbital_index[:, None] == orbital_index[None, :], 1, symmetric).astype(jnp.int32)


def with_spikes(values, key, source, target, parts, factor):
    owner, partner = [(jnp.arange(values.shape[position]) // (values.shape[position] // parts)).reshape([-1 if axis == position else 1 for axis in range(values.ndim)]) for position in (source, target)]
    chosen = jax.random.permutation(key, parts)[partner]
    strong = (owner == chosen) | (owner == (partner + parts // 2) % parts)
    return jnp.where(strong, factor * values, values)


def steps_of(key, shape, cuts, least, top_value):
    def one(position, parts):
        heights = jax.random.uniform(jax.random.fold_in(jax.random.fold_in(key, 6), position), (parts,), jnp.float32, least / len(cuts), top_value / len(cuts))
        return jnp.repeat(jnp.exp(heights), shape[position] // parts).reshape((-1,) + (1,) * (len(shape) - position - 1))

    loudness = one(*cuts[0])
    for cut in cuts[1:]:
        loudness = loudness * one(*cut)
    return loudness


def bell_draw_with(own_key, shape, width, bound, cuts, heavy, kind=jnp.bfloat16):
    result = width * jax.random.normal(own_key, shape, jnp.float32)
    if cuts:
        result = result * steps_of(own_key, shape, cuts, -0.22, 0.18)
    return jnp.clip(with_spikes(result, jax.random.fold_in(own_key, 3), *heavy), -bound, bound).astype(kind)


def setup_inputs(seed: int = 0) -> dict:
    seeds = jax.random.split(jax.random.key(seed), 5)
    three_center = bell_draw_with(seeds[0], (NAUX, NOCC, VIR), (NAUX ** -0.25), 1.0, ((0, 64), (1, 4)), (0, 2, 64, 4.0), jnp.float32)
    occ_energy = jnp.clip(-1.5 + 1.2 * jax.random.uniform(seeds[1], (NOCC,), jnp.float32) ** steps_of(seeds[1], (NOCC,), ((0, 4),), -0.2, 0.2), -1.5, -0.3)
    vir_energy = jnp.clip(jax.random.uniform(seeds[2], (VIR,), jnp.float32, 0.2, 3.0), 0.2, 3.0)
    pair_mask = draw_pair_mask(jax.random.fold_in(seeds[4], 71), 0)
    return {"three_center": three_center, "occ_energy": occ_energy, "vir_energy": vir_energy, "pair_mask": pair_mask}


def reference(three_center, occ_energy, vir_energy, pair_mask):
    aux_total, occ_total, vir_total = three_center.shape
    flat_cols = occ_total * vir_total
    flattened = three_center.reshape(aux_total, flat_cols)
    pair_ints = jnp.dot(flattened.T, flattened, precision=lax.Precision.HIGHEST, preferred_element_type=jnp.float32)
    pair_ints = pair_ints.reshape(occ_total, vir_total, occ_total, vir_total)
    denominator = (vir_energy[None, :, None, None] + vir_energy[None, None, None, :]
                   - occ_energy[:, None, None, None] - occ_energy[None, None, :, None])
    weights = pair_mask.astype(jnp.float32)[:, None, :, None]
    amplitudes = (weights * pair_ints) / denominator
    amplitudes = amplitudes.reshape(flat_cols, flat_cols)
    gamma_aux = jnp.dot(flattened, amplitudes.T, precision=lax.Precision.HIGHEST, preferred_element_type=jnp.float32)
    return gamma_aux.reshape(aux_total, occ_total, vir_total)
```

```python
import functools

import jax
import jax.numpy as jnp
from jax import lax
from jax.experimental import pallas as pl
from jax.experimental.pallas import tpu as pltpu
from jax.sharding import PartitionSpec as P

MESH = pl.DeviceIdType.MESH
f32 = jnp.float32
bf16 = jnp.bfloat16

NQ = 1024
V = 384
QT = 256
OWNERS = 6


def split(value):
    high = value.astype(bf16)
    return high, (value - high.astype(f32)).astype(bf16)


def gram(left, right):
    return lax.dot_general(
        left, right, (((0,), (0,)), ((), ())), preferred_element_type=f32
    )


def kernel(
    own, occ, vir, mask, out,
    nb, hp, lp, part, r1, r2, r3, r4, tot, amp, ah, al, acc, oc, vcol,
    bs, br, os_, or_, js, jr,
):
    y = lax.axis_index("pair")
    aux = lax.axis_index("aux")
    core = lax.rem(aux, 2)
    x = lax.rem(aux // 2, 4)
    z = aux // 8
    up, down, far = (lax.rem(y + d, 4) for d in (1, 3, 2))

    def at_x(d):
        return {"aux": (z * 4 + lax.rem(x + d, 4)) * 2 + core}

    def at_z(d):
        return {"aux": (lax.rem(z + d, 8) * 4 + x) * 2 + core}

    sibling = {"aux": aux + 1 - 2 * core}

    def remote(src, dst, send, recv, device):
        return pltpu.make_async_remote_copy(
            src, dst, send, recv, device_id=device, device_id_type=MESH
        )

    def wait_bytes(ref, sem):
        pltpu.make_async_copy(ref, ref, sem).wait()

    barrier = pltpu.get_barrier_semaphore()
    partners = [{"pair": t} for t in (up, down, far)]
    partners += [at_x(d) for d in (1, 2, 3)] + [at_z(d) for d in range(1, 8)] + [sibling]
    for partner in partners:
        pl.semaphore_signal(barrier, 1, device_id=partner, device_id_type=MESH)
    pl.semaphore_wait(barrier, len(partners))

    oc[y] = jnp.full((8, 128), occ[0], f32)
    for i, t in enumerate((up, down, far)):
        remote(oc.at[y], oc.at[y], os_.at[i], or_.at[0], {"pair": t}).start()

    def wanted(node):
        return lax.rem(node, 4) // 2

    def bulk(k, direction):
        if direction == 0:
            first, relay = wanted(y + 2), wanted(y + 1)
            src, dst, q = (
                (own, 0, first), (own, 0, 1 - first), (nb.at[0], 2, relay),
                (own, 0, 2), (own, 0, 3), (nb.at[0], 2, 1 - relay),
            )[k]
        else:
            first, relay = 2 + wanted(y + 2), 2 + wanted(y + 3)
            src, dst, q = (
                (own, 1, first), (own, 1, 5 - first), (nb.at[1], 2, relay),
                (own, 1, 0), (own, 1, 1), (nb.at[1], 2, 5 - relay),
            )[k]
        rows = pl.ds(pl.multiple_of(q * (3 * QT), 8), 3 * QT)
        return remote(
            src.at[rows], nb.at[dst, rows], bs.at[direction, k], br.at[direction, k],
            {"pair": up if direction == 0 else down},
        )

    def send(k):
        for d in (0, 1):
            bulk(k, d).start()

    def arrive(k):
        for d in (0, 1):
            bulk(k, d).wait_recv()

    def convert(slot, src, q):
        block = src.at[pl.ds(pl.multiple_of(q * (3 * QT), 8), 3 * QT)]
        rows = pl.ds(pl.multiple_of(q * QT, QT), QT)
        for c in range(3):
            high, low = split(block[pl.ds(c, QT, stride=3), :])
            hp[slot, rows, c * 128 : (c + 1) * 128] = high
            lp[slot, rows, c * 128 : (c + 1) * 128] = low

    def contract(t, left, right, q, first):
        rows = pl.ds(pl.multiple_of(q * QT, QT), QT)
        lh, ll, rh, rl = hp[left, rows], lp[left, rows], hp[right, rows], lp[right, rows]
        value = gram(lh, rh) + gram(lh, rl) + gram(ll, rh)
        part[t] = value if first else part[t] + value

    half = pl.multiple_of(core * 192, 8)
    other = pl.multiple_of((1 - core) * 192, 8)
    mine_x = pl.multiple_of(half + x * 48, 8)
    mine = pl.multiple_of(mine_x + z * 8, 8)
    jobs = {"D": (0, 0, 1), "E": (1, 1, 2), "F": (2, 3, 1)}
    owner = z < OWNERS

    def core_sum(name, begin):
        j, b, n = jobs[name]
        copy = remote(
            part.at[pl.ds(b, n), pl.ds(other, 192)], r1.at[pl.ds(b, n)], js.at[j, 0], jr.at[j, 0], sibling
        )
        if begin:
            copy.start()
        else:
            copy.wait_recv()
            part[b : b + n, pl.ds(half, 192)] += r1[b : b + n]

    def x_sum(name, begin):
        j, b, n = jobs[name]
        if begin:
            for d in (2, 1, 3):
                rows = pl.ds(pl.multiple_of(half + lax.rem(x + d, 4) * 48, 8), 48)
                remote(
                    part.at[pl.ds(b, n), rows], r2.at[d - 1, pl.ds(b, n)], js.at[j, 1], jr.at[j, 1], at_x(d)
                ).start()
        else:
            wait_bytes(r2.at[:, pl.ds(b, n)], jr.at[j, 1])
            part[b : b + n, pl.ds(mine_x, 48)] += (
                r2[0, b : b + n] + r2[1, b : b + n] + r2[2, b : b + n]
            )

    def z_sum(name, begin):
        j, b, n = jobs[name]
        if begin:
            for d in (4, 3, 5, 2, 6, 1, 7):
                zd = lax.rem(z + d, 8)

                @pl.when(zd < OWNERS)
                def _():
                    rows = pl.ds(pl.multiple_of(mine_x + zd * 8, 8), 8)
                    remote(
                        part.at[pl.ds(b, n), rows], r3.at[d - 1, pl.ds(b, n)], js.at[j, 2], jr.at[j, 2], at_z(d)
                    ).start()
        else:

            @pl.when(owner)
            def _():
                wait_bytes(r3.at[:, pl.ds(b, n)], jr.at[j, 2])
                value = part[b : b + n, pl.ds(mine, 8)]
                for d in range(7):
                    value += r3[d, b : b + n]
                tot[b : b + n] = value

    def y_sum(name, begin):
        j = jobs[name][0]
        moves = {"E": ((1, 2, down, 3), (2, 1, up, 4)), "F": ((3, 3, far, 3),)}[name]

        @pl.when(owner)
        def _():
            for src, dst, t, s in moves:
                copy = remote(tot.at[src], r4.at[dst], js.at[j, s], jr.at[j, s], {"pair": t})
                if begin:
                    copy.start()
                else:
                    copy.wait_recv()

    low_far = lax.rem(y, 2)
    sides = {0: (y, y), 1: (down, y), 2: (y, up), 3: (low_far, low_far + 2)}

    def scale(name):
        _, b, n = jobs[name]

        @pl.when(owner)
        def _():
            for t in range(b, b + n):
                p, r = sides[t]
                denominator = (vcol[pl.ds(mine, 8), 0:1] + vir[...]) - oc[p, 0:1, 0:1] - oc[r, 0:1, 0:1]
                weight = mask[p, r].astype(f32)
                total = tot[t] + r4[t] if t else tot[t]
                amp[t, pl.ds(mine, 8)] = (weight * total) / denominator

    def z_gather(name, begin):
        j, b, n = jobs[name]
        if begin:

            @pl.when(owner)
            def _():
                ref = amp.at[pl.ds(b, n), pl.ds(mine, 8)]
                for d in (4, 3, 5, 2, 6, 1, 7):
                    remote(ref, ref, js.at[j, 5], jr.at[j, 5], at_z(d)).start()
        else:

            @pl.when(owner)
            def _():
                wait_bytes(amp.at[pl.ds(b, n), pl.ds(mine_x, 40)], jr.at[j, 5])

            @pl.when(jnp.logical_not(owner))
            def _():
                wait_bytes(amp.at[pl.ds(b, n), pl.ds(mine_x, 48)], jr.at[j, 5])

    def x_gather(name, begin):
        j, b, n = jobs[name]
        if begin:
            ref = amp.at[pl.ds(b, n), pl.ds(mine_x, 48)]
            for d in (2, 1, 3):
                remote(ref, ref, js.at[j, 6], jr.at[j, 6], at_x(d)).start()
        else:
            wait_bytes(amp.at[pl.ds(b, n), pl.ds(half, 144)], jr.at[j, 6])

    def core_gather(name, begin):
        j, b, n = jobs[name]
        ref = amp.at[pl.ds(b, n), pl.ds(half, 192)]
        copy = remote(ref, ref, js.at[j, 7], jr.at[j, 7], sibling)
        if begin:
            copy.start()
        else:
            wait_bytes(amp.at[pl.ds(b, n), pl.ds(other, 192)], jr.at[j, 7])

    def factor(slot, turned):
        value = amp[slot]
        ah[slot], al[slot] = split(value.T if turned else value)

    def back(slot, rows):
        high = hp[slot, rows]
        value = jnp.dot(high, ah[slot], preferred_element_type=f32)
        value += jnp.dot(high, al[slot], preferred_element_type=f32)
        return value + jnp.dot(lp[slot, rows], ah[slot], preferred_element_type=f32)

    def quarters(body):
        def step(q, carry):
            body(q, pl.ds(pl.multiple_of(q * QT, QT), QT))
            return carry

        lax.fori_loop(0, 4, step, 0)

    q_far = wanted(y)

    send(0)
    send(1)
    vcol[...] = jnp.broadcast_to(vir[...], (128, V)).T

    part[0] = jnp.zeros((V, V), f32)

    def own_step(q, rows):
        convert(0, own, q)
        contract(0, 0, 0, q, False)

    quarters(own_step)
    core_sum("D", True)
    wait_bytes(oc.at[pl.ds(0, 3)], or_.at[0])
    core_sum("D", False)
    x_sum("D", True)
    arrive(0)
    send(2)
    x_sum("D", False)
    z_sum("D", True)
    first_up, first_down = wanted(y + 1), 2 + wanted(y + 3)
    convert(1, nb.at[0], first_up)
    convert(2, nb.at[1], first_down)
    contract(1, 1, 0, first_up, True)
    contract(2, 0, 2, first_down, True)
    z_sum("D", False)
    scale("D")
    z_gather("D", True)
    arrive(1)
    send(3)
    convert(1, nb.at[0], 1 - first_up)
    convert(2, nb.at[1], 5 - first_down)
    contract(1, 1, 0, 1 - first_up, False)
    contract(2, 0, 2, 5 - first_down, False)
    core_sum("E", True)
    z_gather("D", False)
    x_gather("D", True)
    core_sum("E", False)
    x_sum("E", True)
    x_gather("D", False)
    core_gather("D", True)
    arrive(2)
    send(4)
    convert(3, nb.at[2], q_far)
    convert(3, nb.at[2], 2 + q_far)
    left = jnp.where(y < 2, 0, 3)
    contract(3, left, 3 - left, q_far, True)
    contract(3, left, 3 - left, 2 + q_far, False)
    core_sum("F", True)
    x_sum("E", False)
    z_sum("E", True)
    core_sum("F", False)
    x_sum("F", True)
    core_gather("D", False)
    factor(0, False)

    def own_back(q, rows):
        acc[rows] = back(0, rows)

    quarters(own_back)
    z_sum("E", False)
    y_sum("E", True)
    x_sum("F", False)
    z_sum("F", True)
    arrive(3)
    convert(1, nb.at[0], 2)
    convert(2, nb.at[1], 0)
    y_sum("E", False)
    scale("E")
    z_gather("E", True)
    z_sum("F", False)
    y_sum("F", True)
    send(5)
    arrive(4)
    convert(1, nb.at[0], 3)
    convert(2, nb.at[1], 1)
    y_sum("F", False)
    scale("F")
    z_gather("F", True)
    z_gather("E", False)
    x_gather("E", True)
    z_gather("F", False)
    x_gather("F", True)
    x_gather("E", False)
    core_gather("E", True)
    arrive(5)
    convert(3, nb.at[2], 1 - q_far)
    convert(3, nb.at[2], 3 - q_far)
    core_gather("E", False)
    factor(1, False)
    factor(2, True)

    def near_back(q, rows):
        acc[rows] += back(1, rows) + back(2, rows)

    quarters(near_back)
    x_gather("F", False)
    core_gather("F", True)
    core_gather("F", False)

    @pl.when(y < 2)
    def _():
        factor(3, True)

    @pl.when(y >= 2)
    def _():
        factor(3, False)

    def far_back(q, rows):
        value = acc[rows] + back(3, rows)
        block = out.at[pl.ds(pl.multiple_of(q * (3 * QT), 8), 3 * QT)]
        for c in range(3):
            block[pl.ds(c, QT, stride=3), :] = value[:, c * 128 : (c + 1) * 128]

    quarters(far_back)

    for k in range(6):
        for d in (0, 1):
            bulk(k, d).wait_send()
    for i in range(3):
        wait_bytes(oc.at[0], os_.at[i])
    for name, (j, b, n) in jobs.items():
        blocks = pl.ds(b, n)
        wait_bytes(r1.at[blocks], js.at[j, 0])
        wait_bytes(r2.at[:, blocks], js.at[j, 1])
        wait_bytes(r2.at[:, blocks], js.at[j, 6])
        wait_bytes(r1.at[blocks], js.at[j, 7])

        @pl.when(owner)
        def _():
            wait_bytes(r3.at[pl.ds(0, OWNERS - 1), blocks], js.at[j, 2])
            wait_bytes(r3.at[:, blocks], js.at[j, 5])
            for s in range(3, 3 + {"D": 0, "E": 2, "F": 1}[name]):
                wait_bytes(tot.at[0], js.at[j, s])

        @pl.when(jnp.logical_not(owner))
        def _():
            wait_bytes(r3.at[pl.ds(0, OWNERS), blocks], js.at[j, 2])


def on_device(three_center, occ_energy, vir_energy, pair_mask):
    flat = three_center.reshape(3 * NQ, 128)
    vmem = pl.BlockSpec(memory_space=pltpu.VMEM)
    smem = pl.BlockSpec(memory_space=pltpu.SMEM)
    dma = pltpu.SemaphoreType.DMA
    result = pl.pallas_call(
        kernel,
        out_shape=jax.ShapeDtypeStruct((3 * NQ, 128), f32),
        in_specs=[vmem, smem, vmem, smem],
        out_specs=vmem,
        scratch_shapes=[
            pltpu.VMEM((3, 3 * NQ, 128), f32),
            pltpu.VMEM((4, NQ, V), bf16),
            pltpu.VMEM((4, NQ, V), bf16),
            pltpu.VMEM((4, V, V), f32),
            pltpu.VMEM((4, 192, V), f32),
            pltpu.VMEM((3, 4, 48, V), f32),
            pltpu.VMEM((7, 4, 8, V), f32),
            pltpu.VMEM((4, 8, V), f32),
            pltpu.VMEM((4, 8, V), f32),
            pltpu.VMEM((4, V, V), f32),
            pltpu.VMEM((4, V, V), bf16),
            pltpu.VMEM((4, V, V), bf16),
            pltpu.VMEM((NQ, V), f32),
            pltpu.VMEM((4, 8, 128), f32),
            pltpu.VMEM((V, 128), f32),
            dma((2, 6)),
            dma((2, 6)),
            dma((3,)),
            dma((1,)),
            dma((3, 8)),
            dma((3, 8)),
        ],
        compiler_params=pltpu.CompilerParams(
            collective_id=0, has_side_effects=True, vmem_limit_bytes=48 << 20
        ),
    )(flat, occ_energy, vir_energy.reshape(1, V), pair_mask)
    return result.reshape(NQ, 1, V)


def solution(mesh):
    in_specs = (P("aux", "pair", None), P("pair"), P(), P())
    out_specs = P("aux", "pair", None)
    return jax.shard_map(
        on_device, mesh=mesh, in_specs=in_specs, out_specs=out_specs, check_vma=False
    )
```

```python
import functools

import jax
import jax.numpy as jnp
from jax import lax
from jax.experimental import pallas as pl
from jax.experimental.pallas import tpu as pltpu
from jax.sharding import PartitionSpec as P

MESH = pl.DeviceIdType.MESH
f32 = jnp.float32
bf16 = jnp.bfloat16

NQ = 1024
V = 384
QT = 256
HALF = 3 * QT // 2
OWNERS = 6


def split(value):
    high = value.astype(bf16)
    return high, (value - high.astype(f32)).astype(bf16)


def gram(left, right):
    return lax.dot_general(
        left, right, (((0,), (0,)), ((), ())), preferred_element_type=f32
    )


def kernel(
    own, occ_hbm, vir_hbm, mask_hbm, out,
    ow, occ, vir, mask, ls, nb, wide, part, r1, r2, r3, r4, tot, amp, fac, acc, oc, vcol, den, weight,
    bs, br, os_, or_, js, jr,
):
    y = lax.axis_index("pair")
    aux = lax.axis_index("aux")
    core = lax.rem(aux, 2)
    x = lax.rem(aux // 2, 4)
    z = aux // 8
    up, down, far = (lax.rem(y + d, 4) for d in (1, 3, 2))

    def at_x(d):
        return {"aux": (z * 4 + lax.rem(x + d, 4)) * 2 + core}

    def at_z(d):
        return {"aux": (lax.rem(z + d, 8) * 4 + x) * 2 + core}

    sibling = {"aux": aux + 1 - 2 * core}

    def remote(src, dst, send, recv, device):
        return pltpu.make_async_remote_copy(
            src, dst, send, recv, device_id=device, device_id_type=MESH
        )

    def wait_bytes(ref, sem):
        pltpu.make_async_copy(ref, ref, sem).wait()

    barrier = pltpu.get_barrier_semaphore()
    partners = [{"pair": t} for t in (up, down, far)]
    partners += [at_x(d) for d in (1, 2, 3)] + [at_z(d) for d in range(1, 8)] + [sibling]
    for partner in partners:
        pl.semaphore_signal(barrier, 1, device_id=partner, device_id_type=MESH)
    local = [
        pltpu.make_async_copy(src, dst, ls.at[i])
        for i, (src, dst) in enumerate(((occ_hbm, occ), (vir_hbm, vir), (mask_hbm, mask), (own, ow)))
    ]
    for copy in local:
        copy.start()
    pl.semaphore_wait(barrier, len(partners))

    local[0].wait()
    oc[y] = jnp.full((8, 128), occ[0], f32)
    for i, t in enumerate((up, down, far)):
        remote(oc.at[y], oc.at[y], os_.at[i], or_.at[0], {"pair": t}).start()

    def wanted(node):
        return lax.rem(node, 4) // 2

    def bulk(k, direction):
        if direction == 0:
            first, relay = wanted(y + 2), wanted(y + 1)
            src, dst, q = (
                (own, 0, first), (own, 0, 1 - first), (nb.at[0], 2, relay),
                (own, 0, 2), (own, 0, 3), (nb.at[0], 2, 1 - relay), (own, 0, 3),
            )[k]
        else:
            first, relay = 2 + wanted(y + 2), 2 + wanted(y + 3)
            src, dst, q = (
                (own, 1, first), (own, 1, 5 - first), (nb.at[1], 2, relay),
                (own, 1, 0), (own, 1, 1), (nb.at[1], 2, 5 - relay), (own, 1, 1),
            )[k]
        skip, size = {4: (0, HALF), 6: (HALF, HALF)}.get(k, (0, 2 * HALF))
        rows = pl.ds(pl.multiple_of(q * (2 * HALF) + skip, 8), size)
        return remote(
            src.at[rows], nb.at[dst, rows], bs.at[direction, k], br.at[direction, k],
            {"pair": up if direction == 0 else down},
        )

    def send(k):
        for d in (0, 1):
            bulk(k, d).start()

    def arrive(k):
        for d in (0, 1):
            bulk(k, d).wait_recv()

    def convert(slot, src, q):
        block = src.at[pl.ds(pl.multiple_of(q * (3 * QT), 8), 3 * QT)]
        rows = pl.ds(pl.multiple_of(q * QT, QT), QT)
        for c in range(3):
            high, low = split(block[pl.ds(c, QT, stride=3), :])
            for start, value in ((0, high), (V, low), (2 * V, high)):
                wide[slot, rows, start + c * 128 : start + (c + 1) * 128] = value

    def contract(t, left, right, q, first):
        rows = pl.ds(pl.multiple_of(q * QT, QT), QT)
        lh, ll = wide[left, rows, 0:V], wide[left, rows, V : 2 * V]
        rh, rl = wide[right, rows, 0:V], wide[right, rows, V : 2 * V]
        value = gram(lh, rh) + gram(lh, rl) + gram(ll, rh)
        part[t] = value if first else part[t] + value

    half = pl.multiple_of(core * 192, 8)
    other = pl.multiple_of((1 - core) * 192, 8)
    mine_x = pl.multiple_of(half + x * 48, 8)
    mine = pl.multiple_of(mine_x + z * 8, 8)
    jobs = {"D": (0, 0, 1), "M": (1, 1, 1), "P": (2, 2, 1), "F": (3, 3, 1)}
    owner = z < OWNERS

    def core_sum(name, begin):
        j, b, n = jobs[name]
        copy = remote(
            part.at[pl.ds(b, n), pl.ds(other, 192)], r1.at[pl.ds(b, n)], js.at[j, 0], jr.at[j, 0], sibling
        )
        if begin:
            copy.start()
        else:
            copy.wait_recv()
            part[b : b + n, pl.ds(half, 192)] += r1[b : b + n]

    def x_sum(name, begin):
        j, b, n = jobs[name]
        if begin:
            for d in (2, 1, 3):
                rows = pl.ds(pl.multiple_of(half + lax.rem(x + d, 4) * 48, 8), 48)
                remote(
                    part.at[pl.ds(b, n), rows], r2.at[d - 1, pl.ds(b, n)], js.at[j, 1], jr.at[j, 1], at_x(d)
                ).start()
        else:
            wait_bytes(r2.at[:, pl.ds(b, n)], jr.at[j, 1])
            part[b : b + n, pl.ds(mine_x, 48)] += (
                r2[0, b : b + n] + r2[1, b : b + n] + r2[2, b : b + n]
            )

    def z_sum(name, begin):
        j, b, n = jobs[name]
        if begin:
            for d in (4, 3, 5, 2, 6, 1, 7):
                zd = lax.rem(z + d, 8)

                @pl.when(zd < OWNERS)
                def _():
                    rows = pl.ds(pl.multiple_of(mine_x + zd * 8, 8), 8)
                    remote(
                        part.at[pl.ds(b, n), rows], r3.at[d - 1, pl.ds(b, n)], js.at[j, 2], jr.at[j, 2], at_z(d)
                    ).start()
        else:

            @pl.when(owner)
            def _():
                wait_bytes(r3.at[:, pl.ds(b, n)], jr.at[j, 2])
                value = part[b : b + n, pl.ds(mine, 8)]
                for d in range(7):
                    value += r3[d, b : b + n]
                tot[b : b + n] = value

    def y_sum(name, begin):
        t, there, partner = {"M": (1, 2, down), "P": (2, 1, up), "F": (3, 3, far)}[name]

        @pl.when(owner)
        def _():
            if begin:
                remote(tot.at[t], r4.at[there], js.at[t, 3], jr.at[there, 3], {"pair": partner}).start()
            else:
                wait_bytes(r4.at[t], jr.at[t, 3])

    low_far = lax.rem(y, 2)
    sides = {0: (y, y), 1: (down, y), 2: (y, up), 3: (low_far, low_far + 2)}

    def scale(name):
        _, b, n = jobs[name]

        @pl.when(owner)
        def _():
            for t in range(b, b + n):
                total = tot[t] + r4[t] if t else tot[t]
                amp[t, pl.ds(mine, 8)] = (weight[t, :, 0:1] * total) / den[t]

    def prepare():
        own_rows = pl.ds(pl.multiple_of(lax.rem(mine, V), 8), 8)
        for t in range(4):
            p, r = sides[t]
            weight[t] = jnp.full((8, 128), mask[p, r].astype(f32))
            den[t] = (vcol[own_rows, 0:1] + vir[...]) - oc[p, 0:1, 0:1] - oc[r, 0:1, 0:1]

    def z_gather(name, begin):
        j, b, n = jobs[name]
        if begin:

            @pl.when(owner)
            def _():
                ref = amp.at[pl.ds(b, n), pl.ds(mine, 8)]
                for d in (4, 3, 5, 2, 6, 1, 7):
                    remote(ref, ref, js.at[j, 5], jr.at[j, 5], at_z(d)).start()
        else:

            @pl.when(owner)
            def _():
                wait_bytes(amp.at[pl.ds(b, n), pl.ds(mine_x, 40)], jr.at[j, 5])

            @pl.when(jnp.logical_not(owner))
            def _():
                wait_bytes(amp.at[pl.ds(b, n), pl.ds(mine_x, 48)], jr.at[j, 5])

    def x_gather(name, begin):
        j, b, n = jobs[name]
        if begin:
            ref = amp.at[pl.ds(b, n), pl.ds(mine_x, 48)]
            for d in (2, 1, 3):
                remote(ref, ref, js.at[j, 6], jr.at[j, 6], at_x(d)).start()
        else:
            wait_bytes(amp.at[pl.ds(b, n), pl.ds(half, 144)], jr.at[j, 6])

    def core_gather(name, begin):
        j, b, n = jobs[name]
        ref = amp.at[pl.ds(b, n), pl.ds(half, 192)]
        copy = remote(ref, ref, js.at[j, 7], jr.at[j, 7], sibling)
        if begin:
            copy.start()
        else:
            wait_bytes(amp.at[pl.ds(b, n), pl.ds(other, 192)], jr.at[j, 7])

    def factor(slot, turned):
        value = amp[slot]
        high, low = split(value.T if turned else value)
        fac[slot, 0:V] = high
        fac[slot, V : 2 * V] = high
        fac[slot, 2 * V :] = low

    def back(slot, rows):
        return jnp.dot(wide[slot, rows], fac[slot], preferred_element_type=f32)

    def quarters(body):
        def step(q, carry):
            body(q, pl.ds(pl.multiple_of(q * QT, QT), QT))
            return carry

        lax.fori_loop(0, 4, step, 0)

    q_far = wanted(y)

    def own_step(q, rows):
        convert(0, ow, q)
        contract(0, 0, 0, q, False)

    def own_back(q, rows):
        acc[rows] = back(0, rows)

    def up_back(q, rows):
        acc[rows] += back(1, rows)

    def down_back(q, rows):
        acc[rows] += back(2, rows)

    def far_back(q, rows):
        value = acc[rows] + back(3, rows)
        block = out.at[pl.ds(pl.multiple_of(q * (3 * QT), 8), 3 * QT)]
        for c in range(3):
            block[pl.ds(c, QT, stride=3), :] = value[:, c * 128 : (c + 1) * 128]

    send(0)
    send(1)
    for copy in local[1:]:
        copy.wait()
    vcol[...] = jnp.broadcast_to(vir[...], (128, V)).T
    part[0] = jnp.zeros((V, V), f32)
    quarters(own_step)
    core_sum("D", True)
    wait_bytes(oc.at[pl.ds(0, 3)], or_.at[0])
    core_sum("D", False)
    x_sum("D", True)
    arrive(0)
    send(2)
    first_up, first_down = wanted(y + 1), 2 + wanted(y + 3)
    convert(1, nb.at[0], first_up)
    contract(1, 1, 0, first_up, True)
    convert(2, nb.at[1], first_down)
    contract(2, 0, 2, first_down, True)
    prepare()
    x_sum("D", False)
    z_sum("D", True)
    z_sum("D", False)
    scale("D")
    z_gather("D", True)
    arrive(1)
    send(3)
    convert(1, nb.at[0], 1 - first_up)
    contract(1, 1, 0, 1 - first_up, False)
    core_sum("M", True)
    convert(2, nb.at[1], 5 - first_down)
    contract(2, 0, 2, 5 - first_down, False)
    core_sum("P", True)
    core_sum("M", False)
    x_sum("M", True)
    core_sum("P", False)
    x_sum("P", True)
    z_gather("D", False)
    arrive(2)
    left = jnp.where(y < 2, 0, 3)
    convert(3, nb.at[2], q_far)
    contract(3, left, 3 - left, q_far, True)
    convert(3, nb.at[2], 2 + q_far)
    contract(3, left, 3 - left, 2 + q_far, False)
    core_sum("F", True)
    x_sum("M", False)
    z_sum("M", True)
    core_sum("F", False)
    x_sum("F", True)
    x_sum("P", False)
    z_sum("P", True)
    x_gather("D", True)
    z_sum("M", False)
    y_sum("M", True)
    send(4)
    x_sum("F", False)
    z_sum("F", True)
    z_sum("P", False)
    y_sum("P", True)
    y_sum("M", False)
    scale("M")
    z_gather("M", True)
    arrive(3)
    convert(1, nb.at[0], 2)
    convert(2, nb.at[1], 0)
    z_sum("F", False)
    y_sum("F", True)
    send(6)
    send(5)
    y_sum("P", False)
    scale("P")
    z_gather("P", True)
    z_gather("M", False)
    x_gather("M", True)
    y_sum("F", False)
    scale("F")
    z_gather("F", True)
    x_gather("D", False)
    core_gather("D", True)
    z_gather("P", False)
    x_gather("P", True)
    core_gather("D", False)
    factor(0, False)
    quarters(own_back)
    z_gather("F", False)
    x_gather("F", True)
    arrive(4)
    arrive(6)
    convert(1, nb.at[0], 3)
    convert(2, nb.at[1], 1)
    x_gather("M", False)
    core_gather("M", True)
    core_gather("M", False)
    factor(1, False)
    x_gather("P", False)
    core_gather("P", True)
    quarters(up_back)
    core_gather("P", False)
    factor(2, True)
    x_gather("F", False)
    core_gather("F", True)
    quarters(down_back)
    arrive(5)
    convert(3, nb.at[2], 1 - q_far)
    convert(3, nb.at[2], 3 - q_far)
    core_gather("F", False)

    @pl.when(y < 2)
    def _():
        factor(3, True)

    @pl.when(y >= 2)
    def _():
        factor(3, False)

    quarters(far_back)

    for k in range(7):
        for d in (0, 1):
            bulk(k, d).wait_send()
    for i in range(3):
        wait_bytes(oc.at[0], os_.at[i])
    for name, (j, b, n) in jobs.items():
        blocks = pl.ds(b, n)
        wait_bytes(r1.at[blocks], js.at[j, 0])
        wait_bytes(r2.at[:, blocks], js.at[j, 1])
        wait_bytes(r2.at[:, blocks], js.at[j, 6])
        wait_bytes(r1.at[blocks], js.at[j, 7])

        @pl.when(owner)
        def _():
            wait_bytes(r3.at[pl.ds(0, OWNERS - 1), blocks], js.at[j, 2])
            wait_bytes(r3.at[:, blocks], js.at[j, 5])
            if name != "D":
                wait_bytes(tot.at[0], js.at[j, 3])

        @pl.when(jnp.logical_not(owner))
        def _():
            wait_bytes(r3.at[pl.ds(0, OWNERS), blocks], js.at[j, 2])


def on_device(three_center, occ_energy, vir_energy, pair_mask):
    flat = three_center.reshape(3 * NQ, 128)
    vmem = pl.BlockSpec(memory_space=pltpu.VMEM)
    hbm = pl.BlockSpec(memory_space=pltpu.HBM)
    dma = pltpu.SemaphoreType.DMA
    result = pl.pallas_call(
        kernel,
        out_shape=jax.ShapeDtypeStruct((3 * NQ, 128), f32),
        in_specs=[hbm] * 4,
        out_specs=vmem,
        scratch_shapes=[
            pltpu.VMEM((3 * NQ, 128), f32),
            pltpu.SMEM((1,), f32),
            pltpu.VMEM((1, V), f32),
            pltpu.SMEM((4, 4), jnp.int32),
            dma((4,)),
            pltpu.VMEM((3, 3 * NQ, 128), f32),
            pltpu.VMEM((4, NQ, 3 * V), bf16),
            pltpu.VMEM((4, V, V), f32),
            pltpu.VMEM((4, 192, V), f32),
            pltpu.VMEM((3, 4, 48, V), f32),
            pltpu.VMEM((7, 4, 8, V), f32),
            pltpu.VMEM((4, 8, V), f32),
            pltpu.VMEM((4, 8, V), f32),
            pltpu.VMEM((4, V, V), f32),
            pltpu.VMEM((4, 3 * V, V), bf16),
            pltpu.VMEM((NQ, V), f32),
            pltpu.VMEM((4, 8, 128), f32),
            pltpu.VMEM((V, 128), f32),
            pltpu.VMEM((4, 8, V), f32),
            pltpu.VMEM((4, 8, 128), f32),
            dma((2, 7)),
            dma((2, 7)),
            dma((3,)),
            dma((1,)),
            dma((4, 8)),
            dma((4, 8)),
        ],
        compiler_params=pltpu.CompilerParams(
            collective_id=0, has_side_effects=True, vmem_limit_bytes=52 << 20
        ),
    )(flat, occ_energy, vir_energy.reshape(1, V), pair_mask)
    return result.reshape(NQ, 1, V)


def solution(mesh):
    in_specs = (P("aux", "pair", None), P("pair"), P(), P())
    out_specs = P("aux", "pair", None)
    return jax.shard_map(
        on_device, mesh=mesh, in_specs=in_specs, out_specs=out_specs, check_vma=False
    )
```

```python
import functools

import jax
import jax.numpy as jnp
from jax import lax
from jax.experimental import pallas as pl
from jax.experimental.pallas import tpu as pltpu
from jax.sharding import PartitionSpec as P

MESH = pl.DeviceIdType.MESH
f32 = jnp.float32
bf16 = jnp.bfloat16

NQ = 1024
V = 384
QT = 256
HALF = 3 * QT // 2
OWNERS = 6


def split(value):
    high = value.astype(bf16)
    return high, (value - high.astype(f32)).astype(bf16)


def gram(left, right):
    return lax.dot_general(
        left, right, (((0,), (0,)), ((), ())), preferred_element_type=f32
    )


def kernel(
    own, occ_hbm, vir_hbm, mask_hbm, out,
    ow, occ, vir, mask, ls, nb, wide, part, r1, r2, r3, r4, tot, amp, fac, acc, oc, vcol, den, weight,
    bs, br, os_, or_, js, jr,
):
    y = lax.axis_index("pair")
    aux = lax.axis_index("aux")
    core = lax.rem(aux, 2)
    x = lax.rem(aux // 2, 4)
    z = aux // 8
    up, down, far = (lax.rem(y + d, 4) for d in (1, 3, 2))

    def at_x(d):
        return {"aux": (z * 4 + lax.rem(x + d, 4)) * 2 + core}

    def at_z(d):
        return {"aux": (lax.rem(z + d, 8) * 4 + x) * 2 + core}

    sibling = {"aux": aux + 1 - 2 * core}

    def remote(src, dst, send, recv, device):
        return pltpu.make_async_remote_copy(
            src, dst, send, recv, device_id=device, device_id_type=MESH
        )

    def wait_bytes(ref, sem):
        pltpu.make_async_copy(ref, ref, sem).wait()

    barrier = pltpu.get_barrier_semaphore()
    partners = [at_z(d) for d in (4, 3, 5, 2, 6, 1, 7)]
    partners += [{"pair": t} for t in (far, up, down)] + [at_x(d) for d in (2, 1, 3)] + [sibling]
    for partner in partners:
        pl.semaphore_signal(barrier, 1, device_id=partner, device_id_type=MESH)
    local = [
        pltpu.make_async_copy(src, dst, ls.at[i])
        for i, (src, dst) in enumerate(((occ_hbm, occ), (vir_hbm, vir), (mask_hbm, mask), (own, ow)))
    ]
    for copy in local:
        copy.start()
    pl.semaphore_wait(barrier, len(partners))

    def wanted(node):
        return lax.rem(node, 4) // 2

    def bulk(k, direction):
        if direction == 0:
            first, relay = wanted(y + 2), wanted(y + 1)
            src, dst, q = (
                (own, 0, first), (own, 0, 1 - first), (nb.at[0], 2, relay),
                (own, 0, 2), (own, 0, 3), (nb.at[0], 2, 1 - relay), (own, 0, 3),
            )[k]
        else:
            first, relay = 2 + wanted(y + 2), 2 + wanted(y + 3)
            src, dst, q = (
                (own, 1, first), (own, 1, 5 - first), (nb.at[1], 2, relay),
                (own, 1, 0), (own, 1, 1), (nb.at[1], 2, 5 - relay), (own, 1, 1),
            )[k]
        skip, size = {4: (0, HALF), 6: (HALF, HALF)}.get(k, (0, 2 * HALF))
        rows = pl.ds(pl.multiple_of(q * (2 * HALF) + skip, 8), size)
        return remote(
            src.at[rows], nb.at[dst, rows], bs.at[direction, k], br.at[direction, k],
            {"pair": up if direction == 0 else down},
        )

    def send(k):
        for d in (0, 1):
            bulk(k, d).start()

    def arrive(k):
        for d in (0, 1):
            bulk(k, d).wait_recv()

    def convert(slot, src, q):
        block = src.at[pl.ds(pl.multiple_of(q * (3 * QT), 8), 3 * QT)]
        rows = pl.ds(pl.multiple_of(q * QT, QT), QT)
        for c in range(3):
            high, low = split(block[pl.ds(c, QT, stride=3), :])
            for start, value in ((0, high), (V, low), (2 * V, high)):
                wide[slot, rows, start + c * 128 : start + (c + 1) * 128] = value

    def contract(t, left, right, q, first):
        rows = pl.ds(pl.multiple_of(q * QT, QT), QT)
        lh, ll = wide[left, rows, 0:V], wide[left, rows, V : 2 * V]
        rh, rl = wide[right, rows, 0:V], wide[right, rows, V : 2 * V]
        value = gram(lh, rh) + gram(lh, rl) + gram(ll, rh)
        part[t] = value if first else part[t] + value

    half = pl.multiple_of(core * 192, 8)
    other = pl.multiple_of((1 - core) * 192, 8)
    mine_x = pl.multiple_of(half + x * 48, 8)
    mine = pl.multiple_of(mine_x + z * 8, 8)
    jobs = {"D": (0, 0, 1), "M": (1, 1, 1), "P": (2, 2, 1), "F": (3, 3, 1)}
    owner = z < OWNERS

    def core_sum(name, begin):
        j, b, n = jobs[name]
        copy = remote(
            part.at[pl.ds(b, n), pl.ds(other, 192)], r1.at[pl.ds(b, n)], js.at[j, 0], jr.at[j, 0], sibling
        )
        if begin:
            copy.start()
        else:
            copy.wait_recv()
            part[b : b + n, pl.ds(half, 192)] += r1[b : b + n]

    def x_sum(name, begin):
        j, b, n = jobs[name]
        if begin:
            for d in (2, 1, 3):
                rows = pl.ds(pl.multiple_of(half + lax.rem(x + d, 4) * 48, 8), 48)
                remote(
                    part.at[pl.ds(b, n), rows], r2.at[d - 1, pl.ds(b, n)], js.at[j, 1], jr.at[j, 1], at_x(d)
                ).start()
        else:
            wait_bytes(r2.at[:, pl.ds(b, n)], jr.at[j, 1])
            part[b : b + n, pl.ds(mine_x, 48)] += (
                r2[0, b : b + n] + r2[1, b : b + n] + r2[2, b : b + n]
            )

    def z_sum(name, begin):
        j, b, n = jobs[name]
        if begin:
            for d in (4, 3, 5, 2, 6, 1, 7):
                zd = lax.rem(z + d, 8)

                @pl.when(zd < OWNERS)
                def _():
                    rows = pl.ds(pl.multiple_of(mine_x + zd * 8, 8), 8)
                    remote(
                        part.at[pl.ds(b, n), rows], r3.at[d - 1, pl.ds(b, n)], js.at[j, 2], jr.at[j, 2], at_z(d)
                    ).start()
        else:

            @pl.when(owner)
            def _():
                wait_bytes(r3.at[:, pl.ds(b, n)], jr.at[j, 2])
                value = part[b : b + n, pl.ds(mine, 8)]
                for d in range(7):
                    value += r3[d, b : b + n]
                tot[b : b + n] = value

    def y_sum(name, begin):
        t, there, partner = {"M": (1, 2, down), "P": (2, 1, up), "F": (3, 3, far)}[name]

        @pl.when(owner)
        def _():
            if begin:
                remote(tot.at[t], r4.at[there], js.at[t, 3], jr.at[there, 3], {"pair": partner}).start()
            else:
                wait_bytes(r4.at[t], jr.at[t, 3])

    low_far = lax.rem(y, 2)
    sides = {0: (y, y), 1: (down, y), 2: (y, up), 3: (low_far, low_far + 2)}

    def scale(name):
        _, b, n = jobs[name]

        @pl.when(owner)
        def _():
            for t in range(b, b + n):
                total = tot[t] + r4[t] if t else tot[t]
                amp[t, pl.ds(mine, 8)] = (weight[t, :, 0:1] * total) / den[t]

    def prepare():
        own_rows = pl.ds(pl.multiple_of(lax.rem(mine, V), 8), 8)
        for t in range(4):
            p, r = sides[t]
            weight[t] = jnp.full((8, 128), mask[p, r].astype(f32))
            den[t] = (vcol[own_rows, 0:1] + vir[...]) - oc[p, 0:1, 0:1] - oc[r, 0:1, 0:1]

    def z_gather(name, begin):
        j, b, n = jobs[name]
        if begin:

            @pl.when(owner)
            def _():
                ref = amp.at[pl.ds(b, n), pl.ds(mine, 8)]
                for d in (4, 3, 5, 2, 6, 1, 7):
                    remote(ref, ref, js.at[j, 5], jr.at[j, 5], at_z(d)).start()
        else:

            @pl.when(owner)
            def _():
                wait_bytes(amp.at[pl.ds(b, n), pl.ds(mine_x, 40)], jr.at[j, 5])

            @pl.when(jnp.logical_not(owner))
            def _():
                wait_bytes(amp.at[pl.ds(b, n), pl.ds(mine_x, 48)], jr.at[j, 5])

    def x_gather(name, begin):
        j, b, n = jobs[name]
        if begin:
            ref = amp.at[pl.ds(b, n), pl.ds(mine_x, 48)]
            for d in (2, 1, 3):
                remote(ref, ref, js.at[j, 6], jr.at[j, 6], at_x(d)).start()
        else:
            wait_bytes(amp.at[pl.ds(b, n), pl.ds(half, 144)], jr.at[j, 6])

    def core_gather(name, begin):
        j, b, n = jobs[name]
        ref = amp.at[pl.ds(b, n), pl.ds(half, 192)]
        copy = remote(ref, ref, js.at[j, 7], jr.at[j, 7], sibling)
        if begin:
            copy.start()
        else:
            wait_bytes(amp.at[pl.ds(b, n), pl.ds(other, 192)], jr.at[j, 7])

    def factor(slot, turned):
        value = amp[slot]
        high, low = split(value.T if turned else value)
        fac[slot, 0:V] = high
        fac[slot, V : 2 * V] = high
        fac[slot, 2 * V :] = low

    def back(slot, rows):
        return jnp.dot(wide[slot, rows], fac[slot], preferred_element_type=f32)

    def quarters(body, low=0, high=4):
        def step(q, carry):
            body(q, pl.ds(pl.multiple_of(q * QT, QT), QT))
            return carry

        lax.fori_loop(low, high, step, 0)

    q_far = wanted(y)

    def own_step(q, rows):
        convert(0, ow, q)
        contract(0, 0, 0, q, False)

    def own_back(q, rows):
        acc[rows] = back(0, rows)

    def up_back(q, rows):
        acc[rows] += back(1, rows)

    def down_back(q, rows):
        acc[rows] += back(2, rows)

    def far_back(q, rows):
        value = acc[rows] + back(3, rows)
        block = out.at[pl.ds(pl.multiple_of(q * (3 * QT), 8), 3 * QT)]
        for c in range(3):
            block[pl.ds(c, QT, stride=3), :] = value[:, c * 128 : (c + 1) * 128]

    local[0].wait()
    oc[y] = jnp.full((8, 128), occ[0], f32)
    for i, t in enumerate((up, down, far)):
        remote(oc.at[y], oc.at[y], os_.at[i], or_.at[0], {"pair": t}).start()
    send(0)
    send(1)
    for copy in local[1:]:
        copy.wait()
    vcol[...] = jnp.broadcast_to(vir[...], (128, V)).T
    part[0] = jnp.zeros((V, V), f32)
    quarters(own_step)
    core_sum("D", True)
    core_sum("D", False)
    x_sum("D", True)
    arrive(0)
    send(2)
    first_up, first_down = wanted(y + 1), 2 + wanted(y + 3)
    convert(1, nb.at[0], first_up)
    contract(1, 1, 0, first_up, True)
    convert(2, nb.at[1], first_down)
    contract(2, 0, 2, first_down, True)
    wait_bytes(oc.at[pl.ds(0, 3)], or_.at[0])
    prepare()
    x_sum("D", False)
    z_sum("D", True)
    z_sum("D", False)
    scale("D")
    z_gather("D", True)
    arrive(1)
    send(3)
    convert(1, nb.at[0], 1 - first_up)
    contract(1, 1, 0, 1 - first_up, False)
    core_sum("M", True)
    convert(2, nb.at[1], 5 - first_down)
    contract(2, 0, 2, 5 - first_down, False)
    core_sum("P", True)
    core_sum("M", False)
    x_sum("M", True)
    core_sum("P", False)
    x_sum("P", True)
    z_gather("D", False)
    arrive(2)
    left = jnp.where(y < 2, 0, 3)
    convert(3, nb.at[2], q_far)
    contract(3, left, 3 - left, q_far, True)
    convert(3, nb.at[2], 2 + q_far)
    contract(3, left, 3 - left, 2 + q_far, False)
    core_sum("F", True)
    x_sum("M", False)
    z_sum("M", True)
    core_sum("F", False)
    x_sum("F", True)
    x_sum("P", False)
    z_sum("P", True)
    z_sum("M", False)
    y_sum("M", True)
    send(4)
    x_sum("F", False)
    z_sum("F", True)
    x_gather("D", True)
    z_sum("P", False)
    y_sum("P", True)
    y_sum("M", False)
    scale("M")
    z_gather("M", True)
    arrive(3)
    convert(1, nb.at[0], 2)
    convert(2, nb.at[1], 0)
    z_sum("F", False)
    y_sum("F", True)
    send(6)
    send(5)
    y_sum("P", False)
    scale("P")
    z_gather("P", True)
    y_sum("F", False)
    scale("F")
    z_gather("F", True)
    z_gather("M", False)
    x_gather("M", True)
    x_gather("D", False)
    core_gather("D", True)
    z_gather("P", False)
    x_gather("P", True)
    core_gather("D", False)
    factor(0, False)
    quarters(own_back)
    z_gather("F", False)
    x_gather("F", True)
    arrive(4)
    arrive(6)
    convert(1, nb.at[0], 3)
    x_gather("M", False)
    core_gather("M", True)
    convert(2, nb.at[1], 1)
    core_gather("M", False)
    factor(1, False)
    quarters(up_back, 0, 2)
    x_gather("P", False)
    core_gather("P", True)
    quarters(up_back, 2, 4)
    core_gather("P", False)
    factor(2, True)
    quarters(down_back, 0, 2)
    x_gather("F", False)
    core_gather("F", True)
    quarters(down_back, 2, 4)
    arrive(5)
    convert(3, nb.at[2], 1 - q_far)
    convert(3, nb.at[2], 3 - q_far)
    core_gather("F", False)

    @pl.when(y < 2)
    def _():
        factor(3, True)

    @pl.when(y >= 2)
    def _():
        factor(3, False)

    quarters(far_back)

    for k in range(7):
        for d in (0, 1):
            bulk(k, d).wait_send()
    for i in range(3):
        wait_bytes(oc.at[0], os_.at[i])
    for name, (j, b, n) in jobs.items():
        blocks = pl.ds(b, n)
        wait_bytes(r1.at[blocks], js.at[j, 0])
        wait_bytes(r2.at[:, blocks], js.at[j, 1])
        wait_bytes(r2.at[:, blocks], js.at[j, 6])
        wait_bytes(r1.at[blocks], js.at[j, 7])

        @pl.when(owner)
        def _():
            wait_bytes(r3.at[pl.ds(0, OWNERS - 1), blocks], js.at[j, 2])
            wait_bytes(r3.at[:, blocks], js.at[j, 5])
            if name != "D":
                wait_bytes(tot.at[0], js.at[j, 3])

        @pl.when(jnp.logical_not(owner))
        def _():
            wait_bytes(r3.at[pl.ds(0, OWNERS), blocks], js.at[j, 2])


def on_device(three_center, occ_energy, vir_energy, pair_mask):
    flat = three_center.reshape(3 * NQ, 128)
    vmem = pl.BlockSpec(memory_space=pltpu.VMEM)
    hbm = pl.BlockSpec(memory_space=pltpu.HBM)
    dma = pltpu.SemaphoreType.DMA
    result = pl.pallas_call(
        kernel,
        out_shape=jax.ShapeDtypeStruct((3 * NQ, 128), f32),
        in_specs=[hbm] * 4,
        out_specs=vmem,
        scratch_shapes=[
            pltpu.VMEM((3 * NQ, 128), f32),
            pltpu.SMEM((1,), f32),
            pltpu.VMEM((1, V), f32),
            pltpu.SMEM((4, 4), jnp.int32),
            dma((4,)),
            pltpu.VMEM((3, 3 * NQ, 128), f32),
            pltpu.VMEM((4, NQ, 3 * V), bf16),
            pltpu.VMEM((4, V, V), f32),
            pltpu.VMEM((4, 192, V), f32),
            pltpu.VMEM((3, 4, 48, V), f32),
            pltpu.VMEM((7, 4, 8, V), f32),
            pltpu.VMEM((4, 8, V), f32),
            pltpu.VMEM((4, 8, V), f32),
            pltpu.VMEM((4, V, V), f32),
            pltpu.VMEM((4, 3 * V, V), bf16),
            pltpu.VMEM((NQ, V), f32),
            pltpu.VMEM((4, 8, 128), f32),
            pltpu.VMEM((V, 128), f32),
            pltpu.VMEM((4, 8, V), f32),
            pltpu.VMEM((4, 8, 128), f32),
            dma((2, 7)),
            dma((2, 7)),
            dma((3,)),
            dma((1,)),
            dma((4, 8)),
            dma((4, 8)),
        ],
        compiler_params=pltpu.CompilerParams(
            collective_id=0, has_side_effects=True, vmem_limit_bytes=52 << 20
        ),
    )(flat, occ_energy, vir_energy.reshape(1, V), pair_mask)
    return result.reshape(NQ, 1, V)


def solution(mesh):
    in_specs = (P("aux", "pair", None), P("pair"), P(), P())
    out_specs = P("aux", "pair", None)
    return jax.shard_map(
        on_device, mesh=mesh, in_specs=in_specs, out_specs=out_specs, check_vma=False
    )
```
